128 devices in a mesh: section: 4 (over x_lo, core), dev: 32 (over x_hi, z, y).
Axes of the slice: x: 4 (x_hi: 2, x_lo: 2; x = x_hi * 2 + x_lo), y: 4, z: 4, core: 2. Of those that a mesh axis runs over, the one named last changes fastest.
Arguments:
- queries: bfloat16 [4, 128, 128, 576], P('section', 'dev'), may hold values from -32 to 32
- res_cache: bfloat16 [4, 64, 4096, 576], P('section', 'dev'), may hold values from -5 to 5
- res_lengths: int32 [4, 64], P('section', 'dev'), may hold values from 2048 to 4096, as said below
- inc_cache: bfloat16 [4, 64, 4096, 576], P('section', None, 'dev'), may hold values from -5 to 5
- inc_lengths: int32 [4, 64], replicated, may hold values from 2048 to 4096, as said below
- matching: int32 [4, 64], replicated, may hold values from 0 to 63, as said below
Outputs:
- attended: bfloat16 [4, 128, 128, 512], P('section', 'dev')
The draws below stay inside these ranges and needn't reach their ends.
Inputs may be any that keep to these rules, and one draw needn't show every extreme that they name: `res_lengths`: in each group some resident request has exactly 4096 live slots. `inc_lengths`: in each prefill group some request has exactly 4096 live slots. `matching`: each row is a permutation of 0 to 63.
All inputs are finite; a program needn't handle non-finite values.
Results may differ from the reference program's by a relative error of at most 0.0034.
Values may be sent and summed in bfloat16 or wider, within the bound.
No kernel may reach another device: no remote copies, remote signals or barrier semaphores. Data moves between devices by JAX's collectives and lax.ppermute only.
A program may use at most 192 MiB of HBM per device.

```python
import jax
import jax.numpy as jnp
from jax import lax

HEADS = 128
KV_RANK = 512
ROPE = 64
L = 4096
RES = 2
INC = 2
BATCH = 64
N_SECTION = 4
N_DEV = 32


def shared_parts(key):
    width_all = KV_RANK + ROPE
    row_count = N_SECTION * N_DEV * (RES + INC)
    anchor = jnp.clip(jax.random.normal(jax.random.fold_in(key, 101), (row_count, width_all), jnp.float32), -4.0, 4.0)
    noise_draw = jnp.clip(jax.random.normal(jax.random.fold_in(key, 102), (row_count, width_all), jnp.float32), -4.0, 4.0)
    second = jnp.clip(anchor + 0.3 * noise_draw, -5.0, 5.0)
    section_keys = jax.random.split(jax.random.fold_in(key, 103), N_SECTION)
    matching = jax.vmap(lambda section_key: jax.random.permutation(section_key, N_DEV * INC))(section_keys)
    shaped = (N_SECTION, N_DEV, RES + INC, width_all)
    return (anchor.reshape(shaped), second.reshape(shaped), matching.astype(jnp.int32))


def cache_base(key, shaped):
    return jnp.clip(jax.random.normal(key, shaped, jnp.float32), -4.0, 4.0)


def length_values(key, item_count):
    values = jax.random.randint(jax.random.fold_in(key, 11), (N_SECTION, item_count), L // 2, L + 1, dtype=jnp.int32)
    spot_index = jax.random.randint(jax.random.fold_in(key, 13), (N_SECTION, 1), 0, item_count, dtype=jnp.int32)
    positions = jnp.arange(item_count, dtype=jnp.int32)[None, :]
    return jnp.where(positions == spot_index, L, values).astype(jnp.int32)


def draw_matching(key, part):
    anchor, second, matching = shared_parts(key)
    return matching


def draw_res_cache(key, part):
    anchor, second, matching = shared_parts(key)
    key = jax.random.fold_in(key, 2)
    width_all = KV_RANK + ROPE
    base_draw = cache_base(key, (N_SECTION, N_DEV * RES, L, width_all))
    base_draw = base_draw.at[:, :, 0].set(anchor[:, :, :RES].reshape(N_SECTION, N_DEV * RES, width_all))
    base_draw = base_draw.at[:, :, 1].set(second[:, :, :RES].reshape(N_SECTION, N_DEV * RES, width_all))
    return base_draw.astype(jnp.bfloat16)


def draw_inc_cache(key, part):
    anchor, second, matching = shared_parts(key)
    key = jax.random.fold_in(key, 3)
    width_all = KV_RANK + ROPE
    base_draw = cache_base(key, (N_SECTION, N_DEV * INC, L, width_all))
    shift_by = -(N_SECTION // 2)
    slot_anchor = jnp.roll(anchor[:, :, RES:].reshape(N_SECTION, N_DEV * INC, width_all), shift_by, axis=0)
    slot_second = jnp.roll(second[:, :, RES:].reshape(N_SECTION, N_DEV * INC, width_all), shift_by, axis=0)
    section_ids = jnp.arange(N_SECTION, dtype=jnp.int32)[:, None]
    base_draw = base_draw.at[section_ids, matching, 0].set(slot_anchor)
    base_draw = base_draw.at[section_ids, matching, 1].set(slot_second)
    return base_draw.astype(jnp.bfloat16)


def draw_queries(key, part):
    key = jax.random.fold_in(key, 4)
    width_all = KV_RANK + ROPE
    row_count = N_DEV * (RES + INC)
    base_draw = jnp.clip(jax.random.normal(key, (N_SECTION, row_count, HEADS, width_all), jnp.float32), -4.0, 4.0)
    return base_draw.astype(jnp.bfloat16)


def draw_res_lengths(key, part):
    key = jax.random.fold_in(key, 7)
    return length_values(key, N_DEV * RES)


def draw_inc_lengths(key, part):
    key = jax.random.fold_in(key, 8)
    return length_values(key, N_DEV * INC)


def setup_inputs(seed: int = 0) -> dict:
    splits = jax.random.split(jax.random.key(seed), 7)
    return {
        "queries": draw_queries(jax.random.fold_in(splits[6], 71), 0),
        "res_cache": draw_res_cache(jax.random.fold_in(splits[6], 71), 0),
        "res_lengths": draw_res_lengths(jax.random.fold_in(splits[6], 71), 0),
        "inc_cache": draw_inc_cache(jax.random.fold_in(splits[6], 71), 0),
        "inc_lengths": draw_inc_lengths(jax.random.fold_in(splits[6], 71), 0),
        "matching": draw_matching(jax.random.fold_in(splits[6], 71), 0),
    }


score_scale = 192.0 ** -0.5


def attend(query_row, cache_rows, length):
    scores = jnp.dot(query_row, cache_rows.T, preferred_element_type=jnp.float32) * score_scale
    live_mask = jnp.arange(cache_rows.shape[0], dtype=jnp.int32) < length
    scores = jnp.where(live_mask[None, :], scores, -1e30)
    row_top = jnp.max(scores, axis=1, keepdims=True)
    weights = jnp.exp(scores - row_top)
    row_total = jnp.sum(weights, axis=1, keepdims=True)
    row_probs = weights.astype(jnp.bfloat16)
    latent = jnp.dot(row_probs, cache_rows[:, :KV_RANK], preferred_element_type=jnp.float32)
    return (latent / row_total).astype(jnp.bfloat16)


def reference(queries, res_cache, res_lengths, inc_cache, inc_lengths, matching):
    width_all = KV_RANK + ROPE
    grouped = queries.reshape(N_SECTION, N_DEV, RES + INC, HEADS, width_all)
    res_queries = grouped[:, :, :RES].reshape(N_SECTION * N_DEV * RES, HEADS, width_all)
    inc_queries = grouped[:, :, RES:].reshape(N_SECTION * N_DEV * INC, HEADS, width_all)
    flat_cache = res_cache.reshape(N_SECTION * N_DEV * RES, L, width_all)
    flat_lengths = res_lengths.reshape(N_SECTION * N_DEV * RES)

    def resident_item(item_index):
        return attend(res_queries[item_index], flat_cache[item_index], flat_lengths[item_index])

    res_out = lax.map(resident_item, jnp.arange(N_SECTION * N_DEV * RES, dtype=jnp.int32))
    half_way = N_SECTION // 2

    def incoming_item(item_index):
        group_id = item_index // BATCH
        slot_id = item_index % BATCH
        source = (group_id + half_way) % N_SECTION
        request = matching[source, slot_id]
        return attend(inc_queries[item_index], inc_cache[source, request], inc_lengths[source, request])

    inc_out = lax.map(incoming_item, jnp.arange(N_SECTION * BATCH, dtype=jnp.int32))
    res_out = res_out.reshape(N_SECTION, N_DEV, RES, HEADS, KV_RANK)
    inc_out = inc_out.reshape(N_SECTION, N_DEV, INC, HEADS, KV_RANK)
    joined = jnp.concatenate([res_out, inc_out], axis=2)
    return joined.reshape(N_SECTION, N_DEV * (RES + INC), HEADS, KV_RANK)
```

```python
import functools

import jax
import jax.numpy as jnp
from jax import lax
from jax.experimental import pallas as pl
from jax.experimental.pallas import tpu as pltpu
from jax.sharding import PartitionSpec as P

KV_RANK = 512
SCALE = 192.0 ** (-0.5)
DEAD = -1e30
RING = 4
STAT_ROWS = 16
AXES = ("section", "dev")
VMEM_LIMIT = 48 * 1024 * 1024


def place(x, z, y, core):
    section = (x % 2) * 2 + core
    dev = ((x % RING) // 2) * 16 + (z % RING) * 4 + (y % RING)
    return section * 32 + dev


def move(block, dx=0, dz=0, dy=0):
    route = [
        (place(x, z, y, core), place(x + dx, z + dz, y + dy, core))
        for x in range(RING)
        for z in range(RING)
        for y in range(RING)
        for core in range(2)
    ]
    return lax.ppermute(block, AXES, route)


def positions():
    section = lax.axis_index("section")
    dev = lax.axis_index("dev")
    x_hi, z, y = dev // 16, (dev // 4) % 4, dev % 4
    x_lo = section // 2
    hi_plus = jnp.where(x_lo == 0, x_hi, 1 - x_hi)
    return jnp.stack([section, x_hi, z, y, hi_plus, 1 - hi_plus]).astype(jnp.int32)


def request_of(meta, matching, half, side, cache_step, query_step):
    x_hi = meta[4 + side]
    if half == 0:
        z, y = (meta[2] + query_step) % RING, (meta[3] + cache_step) % RING
    else:
        z, y = (meta[2] + cache_step) % RING, (meta[3] + query_step) % RING
    return matching[meta[0], (x_hi * 16 + z * 4 + y) * 2 + half]


def gather_kernel(steps, meta, matching, cache, *rest):
    outs, sems = rest[:-1], rest[-1]
    copies = []
    slot = 0
    for out, (half, step) in zip(outs, steps):
        for query_step in range(RING):
            for side in range(2):
                request = request_of(meta, matching, half, side, step, query_step)
                copy = pltpu.make_async_copy(
                    cache.at[request], out.at[query_step * 2 + side], sems.at[slot]
                )
                copy.start()
                copies.append(copy)
                slot += 1
    for copy in copies:
        copy.wait()


def gather_requests(steps, meta, matching, cache):
    width, span = cache.shape[1:]
    shape = jax.ShapeDtypeStruct((2 * RING, width, span), cache.dtype)
    size = len(steps) * 2 * RING * width * span * 4
    return pl.pallas_call(
        functools.partial(gather_kernel, steps),
        out_shape=[shape] * len(steps),
        grid_spec=pltpu.PrefetchScalarGridSpec(
            num_scalar_prefetch=2,
            grid=(1,),
            in_specs=[pl.BlockSpec(memory_space=pl.ANY)],
            out_specs=[pl.BlockSpec(memory_space=pl.ANY)] * len(steps),
            scratch_shapes=[pltpu.SemaphoreType.DMA((len(steps) * 2 * RING,))],
        ),
        compiler_params=pltpu.CompilerParams(vmem_limit_bytes=VMEM_LIMIT),
        cost_estimate=pl.CostEstimate(flops=0, bytes_accessed=size, transcendentals=0),
        name="gather_requests",
    )(meta, matching, cache)


def attend_block(query, keys, live):
    scores = jnp.dot(query, keys, preferred_element_type=jnp.float32) * SCALE
    scores = jnp.where(live, scores, DEAD)
    top = jnp.max(scores, axis=1, keepdims=True)
    weights = jnp.exp(scores - top)
    total = jnp.sum(weights, axis=1, keepdims=True)
    mixed = lax.dot_general(
        weights.astype(jnp.bfloat16),
        keys[:KV_RANK],
        (((1,), (1,)), ((), ())),
        preferred_element_type=jnp.float32,
    )
    return mixed / total, top + jnp.log(total)


def resident_kernel(lengths, query, keys, out):
    item = pl.program_id(0)
    live = lax.broadcasted_iota(jnp.int32, (1, keys.shape[2]), 1) < lengths[item]
    mixed, _ = attend_block(query[0].T, keys[0], live)
    out[0] = mixed.astype(jnp.bfloat16)


def resident_rows(lengths, queries, cache):
    count, width, span = cache.shape
    heads = queries.shape[2]
    return pl.pallas_call(
        resident_kernel,
        out_shape=jax.ShapeDtypeStruct((queries.shape[0], heads, KV_RANK), jnp.bfloat16),
        grid_spec=pltpu.PrefetchScalarGridSpec(
            num_scalar_prefetch=1,
            grid=(count,),
            in_specs=[
                pl.BlockSpec((1, width, heads), lambda i, lengths: (i, 0, 0)),
                pl.BlockSpec((1, width, span), lambda i, lengths: (i, 0, 0)),
            ],
            out_specs=pl.BlockSpec((1, heads, KV_RANK), lambda i, lengths: (i, 0, 0)),
        ),
        compiler_params=pltpu.CompilerParams(vmem_limit_bytes=VMEM_LIMIT),
        cost_estimate=pl.CostEstimate(
            flops=2 * count * heads * span * (width + KV_RANK),
            bytes_accessed=2 * count * width * span,
            transcendentals=count * heads * span,
        ),
        name="resident_rows",
    )(lengths, queries, cache)


def split_stat(row):
    high = row.astype(jnp.bfloat16).astype(jnp.float32)
    rest = row - high
    middle = rest.astype(jnp.bfloat16).astype(jnp.float32)
    return high, middle, rest - middle


def put_stat(out, index, row):
    heads = row.shape[1]
    high, middle, low = split_stat(row)
    rows = lax.broadcasted_iota(jnp.int32, (STAT_ROWS, heads), 0)
    block = jnp.where(rows == 0, high, jnp.where(rows == 1, middle, jnp.where(rows == 2, low, 0.0)))
    out[index, heads:, :heads] = block.astype(jnp.bfloat16)
    out[index, heads:, heads:] = jnp.zeros((STAT_ROWS, KV_RANK - heads), jnp.bfloat16)


def partial_kernel(half, meta, matching, lengths, q0, q1, q2, q3, near_a, near_b, k1, k2, k3, o0, o1, o2, o3, query):
    query_step = pl.program_id(0)
    heads = query.shape[1]
    for step, source in enumerate((q0, q1, q2, q3)):

        @pl.when(query_step == step)
        def _():
            query[0] = source[0].T
            query[1] = source[1].T

    span = near_a.shape[2]
    lane = lax.broadcasted_iota(jnp.int32, (1, span), 1)
    slots = []
    for step in range(RING):
        z, y = meta[2], meta[3]
        if half == 0:
            y = (y + RING - step) % RING
        else:
            z = (z + RING - step) % RING
        slots.append(lane + (meta[1] * 16 + z * 4 + y) * span)
    slots = jnp.concatenate(slots, axis=1)
    results = []
    for side, near in enumerate((near_a, near_b)):
        request = request_of(meta, matching, half, side, 0, query_step)
        live = slots < lengths[meta[0], request]
        keys = jnp.concatenate([near[0], k1[side], k2[side], k3[side]], axis=1)
        mixed, stat = attend_block(query[side], keys, live)
        stat_row = jnp.broadcast_to(stat, (heads, heads)).T[:1]
        results.append((mixed.astype(jnp.bfloat16), stat_row))
    for step, out in enumerate((o0, o1, o2, o3)):

        @pl.when(query_step == step)
        def _():
            for side, (mixed, stat_row) in enumerate(results):
                out[side, :heads] = mixed
                put_stat(out, side, stat_row)


def partials(half, meta, matching, lengths, queries, cache, arrived):
    width, span = cache.shape[1:]
    heads = queries[0].shape[2]
    whole_query = pl.BlockSpec((2, width, heads), lambda i, *_: (0, 0, 0))

    def near(side):
        return pl.BlockSpec(
            (1, width, span),
            lambda i, meta, matching, lengths: (request_of(meta, matching, half, side, 0, i), 0, 0),
        )

    far = pl.BlockSpec((2, width, span), lambda i, *_: (i, 0, 0))
    out_block = pl.BlockSpec((2, heads + STAT_ROWS, KV_RANK), lambda i, *_: (0, 0, 0))
    shape = jax.ShapeDtypeStruct((2, heads + STAT_ROWS, KV_RANK), jnp.bfloat16)
    work = 2 * RING * heads * RING * span
    return pl.pallas_call(
        functools.partial(partial_kernel, half),
        out_shape=[shape] * RING,
        grid_spec=pltpu.PrefetchScalarGridSpec(
            num_scalar_prefetch=3,
            grid=(RING,),
            in_specs=[whole_query] * RING + [near(0), near(1)] + [far] * 3,
            out_specs=[out_block] * RING,
            scratch_shapes=[pltpu.VMEM((2, heads, width), jnp.bfloat16)],
        ),
        compiler_params=pltpu.CompilerParams(vmem_limit_bytes=VMEM_LIMIT),
        cost_estimate=pl.CostEstimate(
            flops=2 * work * (width + KV_RANK),
            bytes_accessed=2 * 2 * RING * RING * width * span,
            transcendentals=work,
        ),
        name="partials",
    )(meta, matching, lengths, *queries, cache, cache, *arrived)


def merge(parts):
    heads = parts[0].shape[0] - STAT_ROWS
    stats = []
    for part in parts:
        rows = part[heads:, :heads].astype(jnp.float32)
        stats.append(rows[0:1] + rows[1:2] + rows[2:3])
    top = functools.reduce(jnp.maximum, stats)
    shares = [jnp.exp(stat - top) for stat in stats]
    total = functools.reduce(jnp.add, shares)
    mixed = 0.0
    for part, share in zip(parts, shares):
        column = jnp.broadcast_to(share / total, (heads, heads)).T[:, :1]
        mixed = mixed + part[:heads].astype(jnp.float32) * column
    return mixed, top + jnp.log(total)


def middle_kernel(*refs):
    ins, outs = refs[: 2 * RING], refs[2 * RING :]
    heads = ins[0].shape[1] - STAT_ROWS
    for half in range(2):
        for side in range(2):
            mixed, stat_row = merge([ref[side] for ref in ins[half * RING : (half + 1) * RING]])
            outs[side][half, :heads] = mixed.astype(jnp.bfloat16)
            put_stat(outs[side], half, stat_row)


def middle(parts):
    shape = jax.ShapeDtypeStruct(parts[0].shape, parts[0].dtype)
    return pl.pallas_call(
        middle_kernel,
        out_shape=[shape] * 2,
        compiler_params=pltpu.CompilerParams(vmem_limit_bytes=VMEM_LIMIT),
        name="middle",
    )(*parts)


def last_kernel(base, plus, minus, out):
    del base
    for half in range(2):
        mixed, _ = merge([plus[half], minus[half]])
        out[half] = mixed.astype(jnp.bfloat16)


def last(base, plus, minus):
    count, heads, rank = base.shape
    whole = pl.BlockSpec(plus.shape, lambda i: (0, 0, 0))
    return pl.pallas_call(
        last_kernel,
        out_shape=jax.ShapeDtypeStruct(base.shape, base.dtype),
        grid=(1,),
        in_specs=[pl.BlockSpec(memory_space=pl.ANY), whole, whole],
        out_specs=pl.BlockSpec((count // 2, heads, rank), lambda i: (1, 0, 0)),
        input_output_aliases={0: 0},
        compiler_params=pltpu.CompilerParams(vmem_limit_bytes=VMEM_LIMIT),
        name="last",
    )(base, plus, minus)


def per_device(queries, res_cache, res_lengths, inc_cache, inc_lengths, matching):
    meta = positions()
    queries = jnp.swapaxes(queries[0], 1, 2)
    res_cache = jnp.swapaxes(res_cache[0], 1, 2)
    inc_cache = jnp.swapaxes(inc_cache[0], 1, 2)

    handed = queries[2:]
    from_minus = move(handed, dx=1)
    from_plus = move(handed, dx=-1)

    a1, a3, b1, b3 = gather_requests(((0, 1), (0, 3), (1, 1), (1, 3)), meta, matching, inc_cache)
    a2, b2 = gather_requests(((0, 2), (1, 2)), meta, matching, inc_cache)
    a1 = move(a1, dy=1)
    b1 = move(b1, dz=1)
    a3 = move(a3, dy=-1)
    b3 = move(b3, dz=-1)
    a2 = move(a2, dy=2)
    b2 = move(b2, dz=2)

    qa = jnp.stack([from_plus[0], from_minus[0]])
    qb = jnp.stack([from_plus[1], from_minus[1]])
    qa_all = [qa] + [move(qa, dz=-step) for step in (1, 2, 3)]
    qb_all = [qb] + [move(qb, dy=-step) for step in (1, 2, 3)]

    base = resident_rows(res_lengths[0], queries, res_cache)

    pa = partials(0, meta, matching, inc_lengths, qa_all, inc_cache, (a1, a2, a3))
    pb = partials(1, meta, matching, inc_lengths, qb_all, inc_cache, (b1, b2, b3))
    pa = [pa[0]] + [move(pa[step], dz=step) for step in (1, 2, 3)]
    pb = [pb[0]] + [move(pb[step], dy=step) for step in (1, 2, 3)]
    to_plus, to_minus = middle(pa + pb)
    plus = move(to_plus, dx=1)
    minus = move(to_minus, dx=-1)
    return last(base, plus, minus)[None]


def solution(mesh):
    placed = (
        P("section", "dev", None, None),
        P("section", "dev", None, None),
        P("section", "dev"),
        P("section", None, "dev", None),
        P(),
        P(),
    )
    return jax.shard_map(
        per_device,
        mesh=mesh,
        in_specs=placed,
        out_specs=P("section", "dev", None, None),
        check_vma=False,
    )
```

```python
import functools

import jax
import jax.numpy as jnp
from jax import lax
from jax.experimental import pallas as pl
from jax.experimental.pallas import tpu as pltpu
from jax.sharding import PartitionSpec as P

KV_RANK = 512
SCALE = 192.0 ** (-0.5)
DEAD = -1e30
RING = 4
STAT_ROWS = 16
AXES = ("section", "dev")
SMALL_VMEM = 16 * 1024 * 1024
GATHER_VMEM = 48 * 1024 * 1024
LARGE_VMEM = 56 * 1024 * 1024


def place(x, z, y, core):
    section = (x % 2) * 2 + core
    dev = ((x % RING) // 2) * 16 + (z % RING) * 4 + (y % RING)
    return section * 32 + dev


def move(block, dx=0, dz=0, dy=0):
    route = [
        (place(x, z, y, core), place(x + dx, z + dz, y + dy, core))
        for x in range(RING)
        for z in range(RING)
        for y in range(RING)
        for core in range(2)
    ]
    return lax.ppermute(block, AXES, route)


def positions():
    section = lax.axis_index("section")
    dev = lax.axis_index("dev")
    x_hi, z, y = dev // 16, (dev // 4) % 4, dev % 4
    x_lo = section // 2
    hi_plus = jnp.where(x_lo == 0, x_hi, 1 - x_hi)
    return jnp.stack([section, x_hi, z, y, hi_plus, 1 - hi_plus]).astype(jnp.int32)


def request_of(meta, matching, half, side, cache_step, query_step):
    x_hi = meta[4 + side]
    if half == 0:
        z, y = (meta[2] + query_step) % RING, (meta[3] + cache_step) % RING
    else:
        z, y = (meta[2] + cache_step) % RING, (meta[3] + query_step) % RING
    return matching[meta[0], (x_hi * 16 + z * 4 + y) * 2 + half]


def gather_kernel(steps, meta, matching, cache, *rest):
    outs, sems = rest[:-1], rest[-1]
    copies = []
    slot = 0
    for out, (half, step) in zip(outs, steps):
        for query_step in range(RING):
            for side in range(2):
                request = request_of(meta, matching, half, side, step, query_step)
                copy = pltpu.make_async_copy(
                    cache.at[request], out.at[query_step * 2 + side], sems.at[slot]
                )
                copy.start()
                copies.append(copy)
                slot += 1
    for copy in copies:
        copy.wait()


def gather_requests(steps, room, meta, matching, cache):
    width, span = cache.shape[1:]
    shape = (2 * RING + room, width, span)
    size = len(steps) * 2 * RING * width * span * 4
    return pl.pallas_call(
        functools.partial(gather_kernel, steps),
        out_shape=[pltpu.VMEM(shape, cache.dtype)] * len(steps),
        grid_spec=pltpu.PrefetchScalarGridSpec(
            num_scalar_prefetch=2,
            grid=(1,),
            in_specs=[pl.BlockSpec(memory_space=pl.ANY)],
            out_specs=[pl.BlockSpec(memory_space=pltpu.VMEM)] * len(steps),
            scratch_shapes=[pltpu.SemaphoreType.DMA((len(steps) * 2 * RING,))],
        ),
        compiler_params=pltpu.CompilerParams(vmem_limit_bytes=GATHER_VMEM),
        cost_estimate=pl.CostEstimate(flops=0, bytes_accessed=size, transcendentals=0),
        name="gather_requests",
    )(meta, matching, cache)


def own_kernel(plus, minus, qa, qb):
    for half, out in enumerate((qa, qb)):
        out[0] = plus[half]
        out[1] = minus[half]


def own_queries(plus, minus):
    return pl.pallas_call(
        own_kernel,
        out_shape=[jax.ShapeDtypeStruct(plus.shape, plus.dtype)] * 2,
        compiler_params=pltpu.CompilerParams(vmem_limit_bytes=SMALL_VMEM),
        name="own_queries",
    )(plus, minus)


def fill_kernel(halves, *refs):
    count = len(halves)
    queries = refs[count : count + 2]
    for half, out in zip(halves, refs[count + 2 :]):
        out[...] = queries[half][...]


def fill_queries(halves, arrays, qa, qb):
    count = len(arrays)
    whole = pl.BlockSpec(qa.shape, lambda i: (0, 0, 0))
    return pl.pallas_call(
        functools.partial(fill_kernel, halves),
        out_shape=[jax.ShapeDtypeStruct(x.shape, x.dtype) for x in arrays],
        grid=(1,),
        in_specs=[pl.BlockSpec(memory_space=pl.ANY)] * count + [whole] * 2,
        out_specs=[pl.BlockSpec(qa.shape, lambda i: (RING, 0, 0))] * count,
        input_output_aliases={i: i for i in range(count)},
        compiler_params=pltpu.CompilerParams(vmem_limit_bytes=SMALL_VMEM),
        name="fill_queries",
    )(*arrays, qa, qb)


def weigh(blocks):
    scores = [
        jnp.dot(query, keys, preferred_element_type=jnp.float32) * SCALE for query, keys, _ in blocks
    ]
    scores = [jnp.where(live, score, DEAD) for score, (_, _, live) in zip(scores, blocks)]
    tops = [jnp.max(score, axis=1, keepdims=True) for score in scores]
    weights = [jnp.exp(score - top) for score, top in zip(scores, tops)]
    totals = [jnp.sum(weight, axis=1, keepdims=True) for weight in weights]
    mixed = [
        lax.dot_general(
            weight.astype(jnp.bfloat16),
            keys[:KV_RANK],
            (((1,), (1,)), ((), ())),
            preferred_element_type=jnp.float32,
        )
        for weight, (_, keys, _) in zip(weights, blocks)
    ]
    return mixed, tops, totals


def resident_kernel(lengths, query, keys, out):
    item = pl.program_id(0)
    live = lax.broadcasted_iota(jnp.int32, (1, keys.shape[2]), 1) < lengths[item]
    (mixed,), _, (total,) = weigh([(query[0].T, keys[0], live)])
    out[0] = (mixed / total).astype(jnp.bfloat16)


def resident_rows(lengths, queries, cache):
    count, width, span = cache.shape
    heads = queries.shape[2]
    return pl.pallas_call(
        resident_kernel,
        out_shape=jax.ShapeDtypeStruct((queries.shape[0], heads, KV_RANK), jnp.bfloat16),
        grid_spec=pltpu.PrefetchScalarGridSpec(
            num_scalar_prefetch=1,
            grid=(count,),
            in_specs=[
                pl.BlockSpec((1, width, heads), lambda i, lengths: (i, 0, 0)),
                pl.BlockSpec((1, width, span), lambda i, lengths: (i, 0, 0)),
            ],
            out_specs=pl.BlockSpec((1, heads, KV_RANK), lambda i, lengths: (i, 0, 0)),
        ),
        compiler_params=pltpu.CompilerParams(vmem_limit_bytes=LARGE_VMEM),
        cost_estimate=pl.CostEstimate(
            flops=2 * count * heads * span * (width + KV_RANK),
            bytes_accessed=2 * count * width * span,
            transcendentals=count * heads * span,
        ),
        name="resident_rows",
    )(lengths, queries, cache)


def split_stat(row):
    high = row.astype(jnp.bfloat16).astype(jnp.float32)
    rest = row - high
    middle = rest.astype(jnp.bfloat16).astype(jnp.float32)
    return high, middle, rest - middle


def put_stat(out, index, row):
    heads = row.shape[1]
    high, middle, low = split_stat(row)
    rows = lax.broadcasted_iota(jnp.int32, (STAT_ROWS, heads), 0)
    block = jnp.where(rows == 0, high, jnp.where(rows == 1, middle, jnp.where(rows == 2, low, 0.0)))
    out[index, heads:, :heads] = block.astype(jnp.bfloat16)
    out[index, heads:, heads:] = jnp.zeros((STAT_ROWS, KV_RANK - heads), jnp.bfloat16)


def slots_of(meta, half, away, span):
    z, y = meta[2], meta[3]
    if half == 0:
        y = (y + RING - away) % RING
    else:
        z = (z + RING - away) % RING
    return lax.broadcasted_iota(jnp.int32, (1, span), 1) + (meta[1] * 16 + z * 4 + y) * span


def ring_results(step, meta, matching, lengths, a, b, queries):
    span = a[0].shape[2]
    blocks = []
    for half, segments in enumerate((a, b)):
        slots = jnp.concatenate([slots_of(meta, half, away, span) for away in range(RING)], axis=1)
        for side in range(2):
            request = request_of(meta, matching, half, side, 0, step)
            live = slots < lengths[meta[0], request]
            keys = jnp.concatenate([segment[2 * step + side] for segment in segments], axis=1)
            blocks.append((queries[half][side].T, keys, live))
    mixed, tops, totals = weigh(blocks)
    return [(m / t, stat_row(top, t)) for m, top, t in zip(mixed, tops, totals)]


def stat_row(top, total):
    heads = top.shape[0]
    return jnp.broadcast_to(top + jnp.log(total), (heads, heads)).T[:1]


def put_results(outs, results):
    for index, (value, row) in enumerate(results):
        half, side = divmod(index, 2)
        heads = value.shape[0]
        outs[half][side, :heads] = value.astype(jnp.bfloat16)
        put_stat(outs[half], side, row)


def partial_kernel(step, meta, matching, lengths, *refs):
    a, b, qa, qb, outs = refs[:RING], refs[RING : 2 * RING], refs[2 * RING], refs[2 * RING + 1], refs[2 * RING + 2 :]
    if step != 2:
        back = RING - step
        qa, qb = b[back].at[2 * RING :], a[back].at[2 * RING :]
    put_results(outs, ring_results(step, meta, matching, lengths, a, b, (qa, qb)))


def ring_call(kernel, operands, arrays, name):
    meta, matching, lengths = operands
    width, span = arrays[0].shape[1:]
    heads = span
    work = 4 * heads * span * RING
    whole = pl.BlockSpec(memory_space=pltpu.VMEM)
    shape = (2, heads + STAT_ROWS, KV_RANK)
    return pl.pallas_call(
        kernel,
        out_shape=[pltpu.VMEM(shape, jnp.bfloat16)] * 2,
        grid_spec=pltpu.PrefetchScalarGridSpec(
            num_scalar_prefetch=3,
            grid=(1,),
            in_specs=[whole] * len(arrays),
            out_specs=[whole] * 2,
        ),
        compiler_params=pltpu.CompilerParams(vmem_limit_bytes=SMALL_VMEM),
        cost_estimate=pl.CostEstimate(
            flops=2 * work * (width + KV_RANK),
            bytes_accessed=8 * RING * width * span,
            transcendentals=work,
        ),
        name=name,
    )(meta, matching, lengths, *arrays)


def merge(parts):
    heads = parts[0][0].shape[0]
    stats = [stat for _, stat in parts]
    top = functools.reduce(jnp.maximum, stats)
    shares = [jnp.exp(stat - top) for stat in stats]
    total = functools.reduce(jnp.add, shares)
    mixed = 0.0
    for (value, _), share in zip(parts, shares):
        column = jnp.broadcast_to(share / total, (heads, heads)).T[:, :1]
        mixed = mixed + value * column
    return mixed, top + jnp.log(total)


def received(block):
    heads = block.shape[0] - STAT_ROWS
    rows = block[heads:, :heads].astype(jnp.float32)
    return block[:heads].astype(jnp.float32), rows[0:1] + rows[1:2] + rows[2:3]


def middle_kernel(meta, matching, lengths, *refs):
    a, b, queries, ins, outs = refs[:RING], refs[RING : 2 * RING], refs[8:10], refs[10:16], refs[16:]
    near = ring_results(0, meta, matching, lengths, a, b, queries)
    for half in range(2):
        for side in range(2):
            parts = [near[2 * half + side]] + [received(ref[side]) for ref in ins[3 * half : 3 * half + 3]]
            mixed, row = merge(parts)
            outs[side][half, : mixed.shape[0]] = mixed.astype(jnp.bfloat16)
            put_stat(outs[side], half, row)


def last_kernel(base, plus, minus, out):
    del base
    for half in range(2):
        mixed, _ = merge([received(plus[half]), received(minus[half])])
        out[half] = mixed.astype(jnp.bfloat16)


def last(base, plus, minus):
    count, heads, rank = base.shape
    whole = pl.BlockSpec(plus.shape, lambda i: (0, 0, 0))
    return pl.pallas_call(
        last_kernel,
        out_shape=jax.ShapeDtypeStruct(base.shape, base.dtype),
        grid=(1,),
        in_specs=[pl.BlockSpec(memory_space=pl.ANY), whole, whole],
        out_specs=pl.BlockSpec((count // 2, heads, rank), lambda i: (1, 0, 0)),
        input_output_aliases={0: 0},
        compiler_params=pltpu.CompilerParams(vmem_limit_bytes=SMALL_VMEM),
        name="last",
    )(base, plus, minus)


def per_device(queries, res_cache, res_lengths, inc_cache, inc_lengths, matching):
    meta = positions()
    queries = jnp.swapaxes(queries[0], 1, 2)
    res_cache = jnp.swapaxes(res_cache[0], 1, 2)
    inc_cache = jnp.swapaxes(inc_cache[0], 1, 2)

    from_minus = move(queries[2:], dx=1)
    from_plus = move(queries[2:], dx=-1)
    a2, b2 = gather_requests(((0, 2), (1, 2)), 0, meta, matching, inc_cache)
    a2 = move(a2, dy=2)
    b2 = move(b2, dz=2)
    qa, qb = own_queries(from_plus, from_minus)
    qa_far = move(qa, dz=2)
    qb_far = move(qb, dy=2)
    sent = gather_requests(((0, 1), (0, 3), (1, 1), (1, 3)), 2, meta, matching, inc_cache)
    a1, a3, b1, b3 = fill_queries((1, 1, 0, 0), sent, qa, qb)
    base = resident_rows(res_lengths[0], queries, res_cache)
    a1, a3, a2, qb_far, base = lax.optimization_barrier((a1, a3, a2, qb_far, base))
    b1, b3, b2, qa_far = lax.optimization_barrier((b1, b3, b2, qa_far))
    a1 = move(a1, dy=1)
    a3 = move(a3, dy=-1)
    b1 = move(b1, dz=1)
    b3 = move(b3, dz=-1)
    a0, b0 = gather_requests(((0, 0), (1, 0)), 0, meta, matching, inc_cache)

    operands = (meta, matching, inc_lengths)
    segments = (a0, a1, a2, a3, b0, b1, b2, b3)
    pa, pb = [], []
    for step in (2, 1, 3):
        found = ring_call(
            functools.partial(partial_kernel, step), operands, (*segments, qa_far, qb_far), "partials"
        )
        pa.append(move(found[0], dz=step))
        pb.append(move(found[1], dy=step))
    to_plus, to_minus = ring_call(middle_kernel, operands, (*segments, qa, qb, *pa, *pb), "middle")
    plus = move(to_plus, dx=1)
    minus = move(to_minus, dx=-1)
    return last(base, plus, minus)[None]


def solution(mesh):
    placed = (
        P("section", "dev", None, None),
        P("section", "dev", None, None),
        P("section", "dev"),
        P("section", None, "dev", None),
        P(),
        P(),
    )
    return jax.shard_map(
        per_device,
        mesh=mesh,
        in_specs=placed,
        out_specs=P("section", "dev", None, None),
        check_vma=False,
    )
```

```python
import functools

import jax
import jax.numpy as jnp
from jax import lax
from jax.experimental import pallas as pl
from jax.experimental.pallas import tpu as pltpu
from jax.sharding import PartitionSpec as P

KV_RANK = 512
SCALE = 192.0 ** (-0.5)
DEAD = -1e30
RING = 4
STAT_ROWS = 16
AXES = ("section", "dev")
SMALL_VMEM = 16 * 1024 * 1024
GATHER_VMEM = 48 * 1024 * 1024
LARGE_VMEM = 46 * 1024 * 1024


def place(x, z, y, core):
    section = (x % 2) * 2 + core
    dev = ((x % RING) // 2) * 16 + (z % RING) * 4 + (y % RING)
    return section * 32 + dev


def move(block, dx=0, dz=0, dy=0):
    route = [
        (place(x, z, y, core), place(x + dx, z + dz, y + dy, core))
        for x in range(RING)
        for z in range(RING)
        for y in range(RING)
        for core in range(2)
    ]
    return lax.ppermute(block, AXES, route)


def positions():
    section = lax.axis_index("section")
    dev = lax.axis_index("dev")
    x_hi, z, y = dev // 16, (dev // 4) % 4, dev % 4
    x_lo = section // 2
    hi_plus = jnp.where(x_lo == 0, x_hi, 1 - x_hi)
    return jnp.stack([section, x_hi, z, y, hi_plus, 1 - hi_plus]).astype(jnp.int32)


def request_of(meta, matching, half, side, cache_step, query_step):
    x_hi = meta[4 + side]
    if half == 0:
        z, y = (meta[2] + query_step) % RING, (meta[3] + cache_step) % RING
    else:
        z, y = (meta[2] + cache_step) % RING, (meta[3] + query_step) % RING
    return matching[meta[0], (x_hi * 16 + z * 4 + y) * 2 + half]


def gather_kernel(steps, meta, matching, cache, *rest):
    outs, sems = rest[:-1], rest[-1]
    copies = []
    slot = 0
    for out, (half, step) in zip(outs, steps):
        for query_step in range(RING):
            for side in range(2):
                request = request_of(meta, matching, half, side, step, query_step)
                copy = pltpu.make_async_copy(
                    cache.at[request], out.at[query_step * 2 + side], sems.at[slot]
                )
                copy.start()
                copies.append(copy)
                slot += 1
    for copy in copies:
        copy.wait()


def gather_requests(steps, room, meta, matching, cache):
    width, span = cache.shape[1:]
    shape = (2 * RING + room, width, span)
    size = len(steps) * 2 * RING * width * span * 4
    return pl.pallas_call(
        functools.partial(gather_kernel, steps),
        out_shape=[pltpu.VMEM(shape, cache.dtype)] * len(steps),
        grid_spec=pltpu.PrefetchScalarGridSpec(
            num_scalar_prefetch=2,
            grid=(1,),
            in_specs=[pl.BlockSpec(memory_space=pl.ANY)],
            out_specs=[pl.BlockSpec(memory_space=pltpu.VMEM)] * len(steps),
            scratch_shapes=[pltpu.SemaphoreType.DMA((len(steps) * 2 * RING,))],
        ),
        compiler_params=pltpu.CompilerParams(vmem_limit_bytes=GATHER_VMEM),
        cost_estimate=pl.CostEstimate(flops=0, bytes_accessed=size, transcendentals=0),
        name="gather_requests",
    )(meta, matching, cache)


def pack_kernel(own, far_a, far_b, out):
    out[:2] = own[...]
    out[2] = far_a[0]
    out[3] = far_b[0]


def pack_queries(queries, far_a, far_b):
    shape = queries.shape[1:]
    single = pl.BlockSpec((1,) + shape, lambda i: (0, 0, 0))
    return pl.pallas_call(
        pack_kernel,
        out_shape=jax.ShapeDtypeStruct((4,) + shape, queries.dtype),
        grid=(1,),
        in_specs=[pl.BlockSpec((2,) + shape, lambda i: (1, 0, 0)), single, single],
        out_specs=pl.BlockSpec((4,) + shape, lambda i: (0, 0, 0)),
        compiler_params=pltpu.CompilerParams(vmem_limit_bytes=SMALL_VMEM),
        name="pack_queries",
    )(queries, far_a, far_b)


def fill_kernel(halves, *refs):
    count = len(halves)
    plus, minus = refs[count : count + 2]
    for half, out in zip(halves, refs[count + 2 :]):
        out[0] = plus[half]
        out[1] = minus[half]


def fill_queries(halves, arrays, plus, minus):
    count = len(arrays)
    shape = arrays[0].shape[1:]
    own = pl.BlockSpec((2,) + shape, lambda i: (0, 0, 0))
    return pl.pallas_call(
        functools.partial(fill_kernel, halves),
        out_shape=[jax.ShapeDtypeStruct(x.shape, x.dtype) for x in arrays],
        grid=(1,),
        in_specs=[pl.BlockSpec(memory_space=pl.ANY)] * count + [own] * 2,
        out_specs=[pl.BlockSpec((2,) + shape, lambda i: (RING, 0, 0))] * count,
        input_output_aliases={i: i for i in range(count)},
        compiler_params=pltpu.CompilerParams(vmem_limit_bytes=SMALL_VMEM),
        name="fill_queries",
    )(*arrays, plus, minus)


def weigh(blocks):
    scores = [
        jnp.dot(query, keys, preferred_element_type=jnp.float32) * SCALE for query, keys, _ in blocks
    ]
    scores = [jnp.where(live, score, DEAD) for score, (_, _, live) in zip(scores, blocks)]
    tops = [jnp.max(score, axis=1, keepdims=True) for score in scores]
    weights = [jnp.exp(score - top) for score, top in zip(scores, tops)]
    totals = [jnp.sum(weight, axis=1, keepdims=True) for weight in weights]
    mixed = [
        lax.dot_general(
            weight.astype(jnp.bfloat16),
            keys[:KV_RANK],
            (((1,), (1,)), ((), ())),
            preferred_element_type=jnp.float32,
        )
        for weight, (_, keys, _) in zip(weights, blocks)
    ]
    return mixed, tops, totals


def resident_kernel(lengths, query, keys, out):
    item = pl.program_id(0)
    live = lax.broadcasted_iota(jnp.int32, (1, keys.shape[2]), 1) < lengths[item]
    (mixed,), _, (total,) = weigh([(query[0].T, keys[0], live)])
    out[0] = (mixed / total).astype(jnp.bfloat16)


def resident_rows(lengths, queries, cache):
    count, width, span = cache.shape
    heads = queries.shape[2]
    return pl.pallas_call(
        resident_kernel,
        out_shape=jax.ShapeDtypeStruct((queries.shape[0], heads, KV_RANK), jnp.bfloat16),
        grid_spec=pltpu.PrefetchScalarGridSpec(
            num_scalar_prefetch=1,
            grid=(count,),
            in_specs=[
                pl.BlockSpec((1, width, heads), lambda i, lengths: (i, 0, 0)),
                pl.BlockSpec((1, width, span), lambda i, lengths: (i, 0, 0)),
            ],
            out_specs=pl.BlockSpec((1, heads, KV_RANK), lambda i, lengths: (i, 0, 0)),
        ),
        compiler_params=pltpu.CompilerParams(vmem_limit_bytes=LARGE_VMEM),
        cost_estimate=pl.CostEstimate(
            flops=2 * count * heads * span * (width + KV_RANK),
            bytes_accessed=2 * count * width * span,
            transcendentals=count * heads * span,
        ),
        name="resident_rows",
    )(lengths, queries, cache)


def split_stat(row):
    high = row.astype(jnp.bfloat16).astype(jnp.float32)
    rest = row - high
    middle = rest.astype(jnp.bfloat16).astype(jnp.float32)
    return high, middle, rest - middle


def put_stat(out, index, row):
    heads = row.shape[1]
    high, middle, low = split_stat(row)
    rows = lax.broadcasted_iota(jnp.int32, (STAT_ROWS, heads), 0)
    block = jnp.where(rows == 0, high, jnp.where(rows == 1, middle, jnp.where(rows == 2, low, 0.0)))
    out[index, heads:, :heads] = block.astype(out.dtype)
    out[index, heads:, heads:] = jnp.zeros((STAT_ROWS, KV_RANK - heads), out.dtype)


def slots_of(meta, half, away, span):
    z, y = meta[2], meta[3]
    if half == 0:
        y = (y + RING - away) % RING
    else:
        z = (z + RING - away) % RING
    return lax.broadcasted_iota(jnp.int32, (1, span), 1) + (meta[1] * 16 + z * 4 + y) * span


def ring_results(step, meta, matching, lengths, a, b, queries):
    span = a[0].shape[2]
    blocks = []
    for half, segments in enumerate((a, b)):
        slots = jnp.concatenate([slots_of(meta, half, away, span) for away in range(RING)], axis=1)
        for side in range(2):
            request = request_of(meta, matching, half, side, 0, step)
            live = slots < lengths[meta[0], request]
            keys = jnp.concatenate([segment[2 * step + side] for segment in segments], axis=1)
            blocks.append((queries[half][side][...].T, keys, live))
    mixed, tops, totals = weigh(blocks)
    return [(m / t, stat_row(top, t)) for m, top, t in zip(mixed, tops, totals)]


def stat_row(top, total):
    heads = top.shape[0]
    return jnp.broadcast_to(top + jnp.log(total), (heads, heads)).T[:1]


def put_results(outs, results):
    for index, (value, row) in enumerate(results):
        half, side = divmod(index, 2)
        heads = value.shape[0]
        outs[half][side, :heads] = value.astype(outs[half].dtype)
        put_stat(outs[half], side, row)


def partial_kernel(step, meta, matching, lengths, *refs):
    a, b, plus, minus, outs = refs[:RING], refs[RING : 2 * RING], refs[8], refs[9], refs[10:]
    if step % 2:
        queries = [[ref.at[2 * RING + side] for side in range(2)] for ref in (b[RING - step], a[RING - step])]
    else:
        queries = [[plus.at[step + half], minus.at[step + half]] for half in range(2)]
    put_results(outs, ring_results(step, meta, matching, lengths, a, b, queries))


def partials(step, meta, matching, lengths, arrays):
    width, span = arrays[0].shape[1:]
    heads = span
    work = 4 * heads * span * RING
    whole = pl.BlockSpec(memory_space=pltpu.VMEM)
    shape = (2, heads + STAT_ROWS, KV_RANK)
    dtype = jnp.bfloat16 if step else jnp.float32
    return pl.pallas_call(
        functools.partial(partial_kernel, step),
        out_shape=[pltpu.VMEM(shape, dtype)] * 2,
        grid_spec=pltpu.PrefetchScalarGridSpec(
            num_scalar_prefetch=3,
            grid=(1,),
            in_specs=[whole] * len(arrays),
            out_specs=[whole] * 2,
        ),
        compiler_params=pltpu.CompilerParams(vmem_limit_bytes=SMALL_VMEM),
        cost_estimate=pl.CostEstimate(
            flops=2 * work * (width + KV_RANK),
            bytes_accessed=8 * RING * width * span,
            transcendentals=work,
        ),
        name="partials",
    )(meta, matching, lengths, *arrays)


def merge(parts):
    heads = parts[0][0].shape[0]
    stats = [stat for _, stat in parts]
    top = functools.reduce(jnp.maximum, stats)
    shares = [jnp.exp(stat - top) for stat in stats]
    total = functools.reduce(jnp.add, shares)
    mixed = 0.0
    for (value, _), share in zip(parts, shares):
        column = jnp.broadcast_to(share / total, (heads, heads)).T[:, :1]
        mixed = mixed + value * column
    return mixed, top + jnp.log(total)


def received(block):
    heads = block.shape[0] - STAT_ROWS
    rows = block[heads:, :heads].astype(jnp.float32)
    return block[:heads].astype(jnp.float32), rows[0:1] + rows[1:2] + rows[2:3]


def middle_kernel(*refs):
    ins, outs = refs[: 2 * RING], refs[2 * RING :]
    for half in range(2):
        for side in range(2):
            mixed, row = merge([received(ref[side]) for ref in ins[half * RING : (half + 1) * RING]])
            outs[side][half, : mixed.shape[0]] = mixed.astype(jnp.bfloat16)
            put_stat(outs[side], half, row)


def middle(parts):
    whole = pl.BlockSpec(memory_space=pltpu.VMEM)
    return pl.pallas_call(
        middle_kernel,
        out_shape=[pltpu.VMEM(parts[-1].shape, jnp.bfloat16)] * 2,
        in_specs=[whole] * (2 * RING),
        out_specs=[whole] * 2,
        compiler_params=pltpu.CompilerParams(vmem_limit_bytes=SMALL_VMEM),
        name="middle",
    )(*parts)


def last_kernel(base, plus, minus, out):
    del base
    for half in range(2):
        mixed, _ = merge([received(plus[half]), received(minus[half])])
        out[half] = mixed.astype(jnp.bfloat16)


def last(base, plus, minus):
    count, heads, rank = base.shape
    whole = pl.BlockSpec(plus.shape, lambda i: (0, 0, 0))
    return pl.pallas_call(
        last_kernel,
        out_shape=jax.ShapeDtypeStruct(base.shape, base.dtype),
        grid=(1,),
        in_specs=[pl.BlockSpec(memory_space=pl.ANY), whole, whole],
        out_specs=pl.BlockSpec((count // 2, heads, rank), lambda i: (1, 0, 0)),
        input_output_aliases={0: 0},
        compiler_params=pltpu.CompilerParams(vmem_limit_bytes=SMALL_VMEM),
        name="last",
    )(base, plus, minus)


def per_device(queries, res_cache, res_lengths, inc_cache, inc_lengths, matching):
    meta = positions()
    queries = jnp.swapaxes(queries[0], 1, 2)
    res_cache = jnp.swapaxes(res_cache[0], 1, 2)
    inc_cache = jnp.swapaxes(inc_cache[0], 1, 2)

    far_a = move(queries[2:3], dz=2)
    far_b = move(queries[3:4], dy=2)
    a2, b2 = gather_requests(((0, 2), (1, 2)), 0, meta, matching, inc_cache)
    a2, b2, far_a, far_b = lax.optimization_barrier((a2, b2, far_a, far_b))
    a2 = move(a2, dy=2)
    b2 = move(b2, dz=2)
    packed = pack_queries(queries, far_a, far_b)
    from_minus = move(packed, dx=1)
    from_plus = move(packed, dx=-1)
    sent = gather_requests(((0, 1), (0, 3), (1, 1), (1, 3)), 2, meta, matching, inc_cache)
    a1, a3, b1, b3 = fill_queries((1, 1, 0, 0), sent, from_plus, from_minus)
    a1 = move(a1, dy=1)
    b1 = move(b1, dz=1)
    a3 = move(a3, dy=-1)
    b3, a2, b2, lengths = lax.optimization_barrier((b3, a2, b2, res_lengths[0]))
    b3 = move(b3, dz=-1)
    base = resident_rows(lengths, queries, res_cache)
    later, base = lax.optimization_barrier((meta, base))
    a0, b0 = gather_requests(((0, 0), (1, 0)), 0, later, matching, inc_cache)

    arrays = (a0, a1, a2, a3, b0, b1, b2, b3, from_plus, from_minus)
    pa, pb = [], []
    order = meta
    for step in (2, 1, 3, 0):
        for_a, for_b = partials(step, order, matching, inc_lengths, arrays)
        order, for_a, for_b = lax.optimization_barrier((order, for_a, for_b))
        pa.append(move(for_a, dz=step) if step else for_a)
        pb.append(move(for_b, dy=step) if step else for_b)
    to_plus, to_minus = middle(pa + pb)
    plus = move(to_plus, dx=1)
    minus = move(to_minus, dx=-1)
    return last(base, plus, minus)[None]


def solution(mesh):
    placed = (
        P("section", "dev", None, None),
        P("section", "dev", None, None),
        P("section", "dev"),
        P("section", None, "dev", None),
        P(),
        P(),
    )
    return jax.shard_map(
        per_device,
        mesh=mesh,
        in_specs=placed,
        out_specs=P("section", "dev", None, None),
        check_vma=False,
    )
```

```python
import functools

import jax
import jax.numpy as jnp
from jax import lax
from jax.experimental import pallas as pl
from jax.experimental.pallas import tpu as pltpu
from jax.sharding import PartitionSpec as P

KV_RANK = 512
SCALE = 192.0 ** (-0.5)
DEAD = -1e30
RING = 4
LAST = RING - 1
STAT_ROWS = 16
AXES = ("section", "dev")
SMALL_VMEM = 16 * 1024 * 1024
GATHER_VMEM = 48 * 1024 * 1024
LARGE_VMEM = 46 * 1024 * 1024


def place(x, z, y, core):
    section = (x % 2) * 2 + core
    dev = ((x % RING) // 2) * 16 + (z % RING) * 4 + (y % RING)
    return section * 32 + dev


def move(block, dx=0, dz=0, dy=0):
    route = [
        (place(x, z, y, core), place(x + dx, z + dz, y + dy, core))
        for x in range(RING)
        for z in range(RING)
        for y in range(RING)
        for core in range(2)
    ]
    return lax.ppermute(block, AXES, route)


def positions():
    section = lax.axis_index("section")
    dev = lax.axis_index("dev")
    x_hi, z, y = dev // 16, (dev // 4) % 4, dev % 4
    x_lo = section // 2
    hi_plus = jnp.where(x_lo == 0, x_hi, 1 - x_hi)
    return jnp.stack([section, x_hi, z, y, hi_plus, 1 - hi_plus]).astype(jnp.int32)


def request_of(meta, matching, half, side, cache_step, query_step):
    x_hi = meta[4 + side]
    if half == 0:
        z, y = (meta[2] + query_step) & LAST, (meta[3] + cache_step) & LAST
    else:
        z, y = (meta[2] + cache_step) & LAST, (meta[3] + query_step) & LAST
    return matching[meta[0], (x_hi * 16 + z * 4 + y) * 2 + half]


def gather_kernel(steps, meta, matching, cache, *rest):
    outs, sems = rest[:-1], rest[-1]
    copies = []
    slot = 0
    for out, (half, step) in zip(outs, steps):
        for query_step in range(RING):
            for side in range(2):
                request = request_of(meta, matching, half, side, step, query_step)
                copy = pltpu.make_async_copy(
                    cache.at[request], out.at[query_step * 2 + side], sems.at[slot]
                )
                copy.start()
                copies.append(copy)
                slot += 1
    for copy in copies:
        copy.wait()


def gather_requests(steps, room, meta, matching, cache):
    width, span = cache.shape[1:]
    shape = (2 * RING + room, width, span)
    size = len(steps) * 2 * RING * width * span * 4
    return pl.pallas_call(
        functools.partial(gather_kernel, steps),
        out_shape=[pltpu.VMEM(shape, cache.dtype)] * len(steps),
        grid_spec=pltpu.PrefetchScalarGridSpec(
            num_scalar_prefetch=2,
            grid=(1,),
            in_specs=[pl.BlockSpec(memory_space=pl.ANY)],
            out_specs=[pl.BlockSpec(memory_space=pltpu.VMEM)] * len(steps),
            scratch_shapes=[pltpu.SemaphoreType.DMA((len(steps) * 2 * RING,))],
        ),
        compiler_params=pltpu.CompilerParams(vmem_limit_bytes=GATHER_VMEM),
        cost_estimate=pl.CostEstimate(flops=0, bytes_accessed=size, transcendentals=0),
        name="gather_requests",
    )(meta, matching, cache)


def pack_kernel(own, far_a, far_b, out):
    out[:2] = own[...]
    out[2] = far_a[0]
    out[3] = far_b[0]


def pack_queries(queries, far_a, far_b):
    shape = queries.shape[1:]
    single = pl.BlockSpec((1,) + shape, lambda i: (0, 0, 0))
    return pl.pallas_call(
        pack_kernel,
        out_shape=jax.ShapeDtypeStruct((4,) + shape, queries.dtype),
        grid=(1,),
        in_specs=[pl.BlockSpec((2,) + shape, lambda i: (1, 0, 0)), single, single],
        out_specs=pl.BlockSpec((4,) + shape, lambda i: (0, 0, 0)),
        compiler_params=pltpu.CompilerParams(vmem_limit_bytes=SMALL_VMEM),
        name="pack_queries",
    )(queries, far_a, far_b)


def fill_kernel(halves, *refs):
    count = len(halves)
    plus, minus = refs[count : count + 2]
    for half, out in zip(halves, refs[count + 2 :]):
        out[0] = plus[half]
        out[1] = minus[half]


def fill_queries(halves, arrays, plus, minus):
    count = len(arrays)
    shape = arrays[0].shape[1:]
    own = pl.BlockSpec((2,) + shape, lambda i: (0, 0, 0))
    return pl.pallas_call(
        functools.partial(fill_kernel, halves),
        out_shape=[jax.ShapeDtypeStruct(x.shape, x.dtype) for x in arrays],
        grid=(1,),
        in_specs=[pl.BlockSpec(memory_space=pl.ANY)] * count + [own] * 2,
        out_specs=[pl.BlockSpec((2,) + shape, lambda i: (RING, 0, 0))] * count,
        input_output_aliases={i: i for i in range(count)},
        compiler_params=pltpu.CompilerParams(vmem_limit_bytes=SMALL_VMEM),
        name="fill_queries",
    )(*arrays, plus, minus)


def weigh(blocks):
    scores = [
        jnp.dot(query, keys, preferred_element_type=jnp.float32) * SCALE + bias for query, keys, bias in blocks
    ]
    tops = [jnp.max(score, axis=1, keepdims=True) for score in scores]
    weights = [jnp.exp(score - top) for score, top in zip(scores, tops)]
    totals = [jnp.sum(weight, axis=1, keepdims=True) for weight in weights]
    mixed = [
        lax.dot_general(
            weight.astype(jnp.bfloat16),
            keys[:KV_RANK],
            (((1,), (1,)), ((), ())),
            preferred_element_type=jnp.float32,
        )
        for weight, (_, keys, _) in zip(weights, blocks)
    ]
    return mixed, tops, totals


def resident_kernel(lengths, query, keys, out):
    item = pl.program_id(0)
    live = lax.broadcasted_iota(jnp.int32, (1, keys.shape[2]), 1) < lengths[item]
    bias = jnp.where(live, 0.0, DEAD)
    (mixed,), _, (total,) = weigh([(query[0].T, keys[0], bias)])
    out[0] = (mixed / total).astype(jnp.bfloat16)


def resident_rows(lengths, queries, cache):
    count, width, span = cache.shape
    heads = queries.shape[2]
    return pl.pallas_call(
        resident_kernel,
        out_shape=jax.ShapeDtypeStruct((queries.shape[0], heads, KV_RANK), jnp.bfloat16),
        grid_spec=pltpu.PrefetchScalarGridSpec(
            num_scalar_prefetch=1,
            grid=(count,),
            in_specs=[
                pl.BlockSpec((1, width, heads), lambda i, lengths: (i, 0, 0)),
                pl.BlockSpec((1, width, span), lambda i, lengths: (i, 0, 0)),
            ],
            out_specs=pl.BlockSpec((1, heads, KV_RANK), lambda i, lengths: (i, 0, 0)),
        ),
        compiler_params=pltpu.CompilerParams(vmem_limit_bytes=LARGE_VMEM),
        cost_estimate=pl.CostEstimate(
            flops=2 * count * heads * span * (width + KV_RANK),
            bytes_accessed=2 * count * width * span,
            transcendentals=count * heads * span,
        ),
        name="resident_rows",
    )(lengths, queries, cache)


def split_stat(row):
    high = row.astype(jnp.bfloat16).astype(jnp.float32)
    rest = row - high
    middle = rest.astype(jnp.bfloat16).astype(jnp.float32)
    return high, middle, rest - middle


def put_stat(out, index, row):
    heads = row.shape[1]
    high, middle, low = split_stat(row)
    rows = lax.broadcasted_iota(jnp.int32, (STAT_ROWS, heads), 0)
    block = jnp.where(rows == 0, high, jnp.where(rows == 1, middle, jnp.where(rows == 2, low, 0.0)))
    out[index, heads:, :heads] = block.astype(out.dtype)
    out[index, heads:, heads:] = jnp.zeros((STAT_ROWS, KV_RANK - heads), out.dtype)


def bias_kernel(span, meta, matching, lengths, bias):
    lane = lax.broadcasted_iota(jnp.int32, (1, span), 1)
    for half in range(2):
        slots = []
        for away in range(RING):
            z, y = meta[2], meta[3]
            if half == 0:
                y = (y + RING - away) & LAST
            else:
                z = (z + RING - away) & LAST
            slots.append(lane + (meta[1] * 16 + z * 4 + y) * span)
        slots = jnp.concatenate(slots, axis=1)
        for step in range(RING):
            for side in range(2):
                request = request_of(meta, matching, half, side, 0, step)
                live = slots < lengths[meta[0], request]
                row = (half * RING + step) * 2 + side
                bias[row : row + 1, :] = jnp.where(live, 0.0, DEAD)


def attention_bias(span, meta, matching, lengths):
    scalars = pl.BlockSpec(memory_space=pltpu.SMEM)
    return pl.pallas_call(
        functools.partial(bias_kernel, span),
        out_shape=pltpu.VMEM((4 * RING, RING * span), jnp.float32),
        in_specs=[scalars] * 3,
        out_specs=pl.BlockSpec(memory_space=pltpu.VMEM),
        compiler_params=pltpu.CompilerParams(vmem_limit_bytes=SMALL_VMEM),
        name="attention_bias",
    )(meta, matching, lengths)


def attend_ring(step, bias, a, b, queries, outs):
    blocks = []
    for half, segments in enumerate((a, b)):
        for side in range(2):
            row = (half * RING + step) * 2 + side
            keys = jnp.concatenate([segment[2 * step + side] for segment in segments], axis=1)
            blocks.append((queries[half][side][...].T, keys, bias[row : row + 1, :]))
    mixed, tops, totals = weigh(blocks)
    for index in range(4):
        half, side = divmod(index, 2)
        out = outs[half]
        heads = mixed[index].shape[0]
        out[side, :heads] = (mixed[index] / totals[index]).astype(out.dtype)
        put_stat(out, side, stat_row(tops[index], totals[index]))


def stat_row(top, total):
    heads = top.shape[0]
    return jnp.broadcast_to(top + jnp.log(total), (heads, heads)).T[:1]


def partial_kernel(step, bias, *refs):
    a, b, plus, minus, outs = refs[:RING], refs[RING : 2 * RING], refs[8], refs[9], refs[10:]
    if step % 2:
        queries = [[ref.at[2 * RING + side] for side in range(2)] for ref in (b[RING - step], a[RING - step])]
    else:
        queries = [[plus.at[step + half], minus.at[step + half]] for half in range(2)]
    attend_ring(step, bias, a, b, queries, outs)


def partials(step, bias, arrays):
    width, span = arrays[0].shape[1:]
    heads = span
    work = 4 * heads * span * RING
    whole = pl.BlockSpec(memory_space=pltpu.VMEM)
    shape = (2, heads + STAT_ROWS, KV_RANK)
    dtype = jnp.bfloat16 if step else jnp.float32
    return pl.pallas_call(
        functools.partial(partial_kernel, step),
        out_shape=[pltpu.VMEM(shape, dtype)] * 2,
        in_specs=[whole] * (1 + len(arrays)),
        out_specs=[whole] * 2,
        compiler_params=pltpu.CompilerParams(vmem_limit_bytes=SMALL_VMEM),
        cost_estimate=pl.CostEstimate(
            flops=2 * work * (width + KV_RANK),
            bytes_accessed=8 * RING * width * span,
            transcendentals=work,
        ),
        name="partials",
    )(bias, *arrays)


def merge(parts):
    heads = parts[0][0].shape[0]
    stats = [stat for _, stat in parts]
    top = functools.reduce(jnp.maximum, stats)
    shares = [jnp.exp(stat - top) for stat in stats]
    total = functools.reduce(jnp.add, shares)
    mixed = 0.0
    for (value, _), share in zip(parts, shares):
        column = jnp.broadcast_to(share / total, (heads, heads)).T[:, :1]
        mixed = mixed + value * column
    return mixed, top + jnp.log(total)


def received(block):
    heads = block.shape[0] - STAT_ROWS
    rows = block[heads:, :heads].astype(jnp.float32)
    return block[:heads].astype(jnp.float32), rows[0:1] + rows[1:2] + rows[2:3]


def middle_kernel(*refs):
    ins, outs = refs[: 2 * RING], refs[2 * RING :]
    for half in range(2):
        for side in range(2):
            mixed, row = merge([received(ref[side]) for ref in ins[half * RING : (half + 1) * RING]])
            outs[side][half, : mixed.shape[0]] = mixed.astype(jnp.bfloat16)
            put_stat(outs[side], half, row)


def middle(parts):
    whole = pl.BlockSpec(memory_space=pltpu.VMEM)
    return pl.pallas_call(
        middle_kernel,
        out_shape=[pltpu.VMEM(parts[-1].shape, jnp.bfloat16)] * 2,
        in_specs=[whole] * (2 * RING),
        out_specs=[whole] * 2,
        compiler_params=pltpu.CompilerParams(vmem_limit_bytes=SMALL_VMEM),
        name="middle",
    )(*parts)


def last_kernel(base, plus, minus, out):
    del base
    for half in range(2):
        mixed, _ = merge([received(plus[half]), received(minus[half])])
        out[half] = mixed.astype(jnp.bfloat16)


def last(base, plus, minus):
    count, heads, rank = base.shape
    whole = pl.BlockSpec(plus.shape, lambda i: (0, 0, 0))
    return pl.pallas_call(
        last_kernel,
        out_shape=jax.ShapeDtypeStruct(base.shape, base.dtype),
        grid=(1,),
        in_specs=[pl.BlockSpec(memory_space=pl.ANY), whole, whole],
        out_specs=pl.BlockSpec((count // 2, heads, rank), lambda i: (1, 0, 0)),
        input_output_aliases={0: 0},
        compiler_params=pltpu.CompilerParams(vmem_limit_bytes=SMALL_VMEM),
        name="last",
    )(base, plus, minus)


def per_device(queries, res_cache, res_lengths, inc_cache, inc_lengths, matching):
    meta = positions()
    queries = jnp.swapaxes(queries[0], 1, 2)
    res_cache = jnp.swapaxes(res_cache[0], 1, 2)
    inc_cache = jnp.swapaxes(inc_cache[0], 1, 2)

    far_a = move(queries[2:3], dz=2)
    far_b = move(queries[3:4], dy=2)
    a2, b2 = gather_requests(((0, 2), (1, 2)), 0, meta, matching, inc_cache)
    a2, b2, far_a, far_b = lax.optimization_barrier((a2, b2, far_a, far_b))
    a2 = move(a2, dy=2)
    b2 = move(b2, dz=2)
    packed = pack_queries(queries, far_a, far_b)
    from_minus = move(packed, dx=1)
    from_plus = move(packed, dx=-1)
    sent = gather_requests(((0, 1), (0, 3), (1, 1), (1, 3)), 2, meta, matching, inc_cache)
    a1, a3, b1, b3 = fill_queries((1, 1, 0, 0), sent, from_plus, from_minus)
    a1 = move(a1, dy=1)
    b1 = move(b1, dz=1)
    a3 = move(a3, dy=-1)
    b3, a2, b2, lengths = lax.optimization_barrier((b3, a2, b2, res_lengths[0]))
    b3 = move(b3, dz=-1)
    base = resident_rows(lengths, queries, res_cache)
    later, base = lax.optimization_barrier((meta, base))
    a0, b0 = gather_requests(((0, 0), (1, 0)), 0, later, matching, inc_cache)

    arrays = (a0, a1, a2, a3, b0, b1, b2, b3, from_plus, from_minus)
    pa, pb = [], []
    order = attention_bias(inc_cache.shape[2], later, matching, inc_lengths)
    for step in (2, 1, 3, 0):
        for_a, for_b = partials(step, order, arrays)
        order, for_a, for_b = lax.optimization_barrier((order, for_a, for_b))
        pa.append(move(for_a, dz=step) if step else for_a)
        pb.append(move(for_b, dy=step) if step else for_b)
    to_plus, to_minus = middle(pa + pb)
    plus = move(to_plus, dx=1)
    minus = move(to_minus, dx=-1)
    return last(base, plus, minus)[None]


def solution(mesh):
    placed = (
        P("section", "dev", None, None),
        P("section", "dev", None, None),
        P("section", "dev"),
        P("section", None, "dev", None),
        P(),
        P(),
    )
    return jax.shard_map(
        per_device,
        mesh=mesh,
        in_specs=placed,
        out_specs=P("section", "dev", None, None),
        check_vma=False,
    )
```

```python
import functools

import jax
import jax.numpy as jnp
from jax import lax
from jax.experimental import pallas as pl
from jax.experimental.pallas import tpu as pltpu
from jax.sharding import PartitionSpec as P

KV_RANK = 512
SCALE = 192.0 ** (-0.5)
DEAD = -1e30
RING = 4
LAST = RING - 1
STAT_ROWS = 16
AXES = ("section", "dev")
SMALL_VMEM = 16 * 1024 * 1024
GATHER_VMEM = 48 * 1024 * 1024
LARGE_VMEM = 46 * 1024 * 1024


def place(x, z, y, core):
    section = (x % 2) * 2 + core
    dev = ((x % RING) // 2) * 16 + (z % RING) * 4 + (y % RING)
    return section * 32 + dev


def move(block, dx=0, dz=0, dy=0):
    route = [
        (place(x, z, y, core), place(x + dx, z + dz, y + dy, core))
        for x in range(RING)
        for z in range(RING)
        for y in range(RING)
        for core in range(2)
    ]
    return lax.ppermute(block, AXES, route)


def positions():
    section = lax.axis_index("section")
    dev = lax.axis_index("dev")
    x_hi, z, y = dev // 16, (dev // 4) % 4, dev % 4
    x_lo = section // 2
    hi_plus = jnp.where(x_lo == 0, x_hi, 1 - x_hi)
    return jnp.stack([section, x_hi, z, y, hi_plus, 1 - hi_plus]).astype(jnp.int32)


def request_of(meta, matching, half, side, cache_step, query_step):
    x_hi = meta[4 + side]
    if half == 0:
        z, y = (meta[2] + query_step) & LAST, (meta[3] + cache_step) & LAST
    else:
        z, y = (meta[2] + cache_step) & LAST, (meta[3] + query_step) & LAST
    return matching[meta[0], (x_hi * 16 + z * 4 + y) * 2 + half]


def gather_kernel(steps, meta, matching, cache, *rest):
    outs, sems = rest[:-1], rest[-1]
    copies = []
    slot = 0
    for out, (half, step) in zip(outs, steps):
        for query_step in range(RING):
            for side in range(2):
                request = request_of(meta, matching, half, side, step, query_step)
                copy = pltpu.make_async_copy(
                    cache.at[request], out.at[query_step * 2 + side], sems.at[slot]
                )
                copy.start()
                copies.append(copy)
                slot += 1
    for copy in copies:
        copy.wait()


def gather_requests(steps, room, meta, matching, cache):
    width, span = cache.shape[1:]
    shape = (2 * RING + room, width, span)
    size = len(steps) * 2 * RING * width * span * 4
    return pl.pallas_call(
        functools.partial(gather_kernel, steps),
        out_shape=[pltpu.VMEM(shape, cache.dtype)] * len(steps),
        grid_spec=pltpu.PrefetchScalarGridSpec(
            num_scalar_prefetch=2,
            grid=(1,),
            in_specs=[pl.BlockSpec(memory_space=pl.ANY)],
            out_specs=[pl.BlockSpec(memory_space=pltpu.VMEM)] * len(steps),
            scratch_shapes=[pltpu.SemaphoreType.DMA((len(steps) * 2 * RING,))],
        ),
        compiler_params=pltpu.CompilerParams(vmem_limit_bytes=GATHER_VMEM),
        cost_estimate=pl.CostEstimate(flops=0, bytes_accessed=size, transcendentals=0),
        name="gather_requests",
    )(meta, matching, cache)


def pack_kernel(own, far_a, far_b, out):
    out[:2] = own[...]
    out[2] = far_a[0]
    out[3] = far_b[0]


def pack_queries(queries, far_a, far_b):
    shape = queries.shape[1:]
    single = pl.BlockSpec((1,) + shape, lambda i: (0, 0, 0))
    return pl.pallas_call(
        pack_kernel,
        out_shape=jax.ShapeDtypeStruct((4,) + shape, queries.dtype),
        grid=(1,),
        in_specs=[pl.BlockSpec((2,) + shape, lambda i: (1, 0, 0)), single, single],
        out_specs=pl.BlockSpec((4,) + shape, lambda i: (0, 0, 0)),
        compiler_params=pltpu.CompilerParams(vmem_limit_bytes=SMALL_VMEM),
        name="pack_queries",
    )(queries, far_a, far_b)


def fill_kernel(halves, *refs):
    count = len(halves)
    plus, minus = refs[count : count + 2]
    for half, out in zip(halves, refs[count + 2 :]):
        out[0] = plus[half]
        out[1] = minus[half]


def fill_queries(halves, arrays, plus, minus):
    count = len(arrays)
    shape = arrays[0].shape[1:]
    own = pl.BlockSpec((2,) + shape, lambda i: (0, 0, 0))
    return pl.pallas_call(
        functools.partial(fill_kernel, halves),
        out_shape=[jax.ShapeDtypeStruct(x.shape, x.dtype) for x in arrays],
        grid=(1,),
        in_specs=[pl.BlockSpec(memory_space=pl.ANY)] * count + [own] * 2,
        out_specs=[pl.BlockSpec((2,) + shape, lambda i: (RING, 0, 0))] * count,
        input_output_aliases={i: i for i in range(count)},
        compiler_params=pltpu.CompilerParams(vmem_limit_bytes=SMALL_VMEM),
        name="fill_queries",
    )(*arrays, plus, minus)


def weigh(blocks):
    scores = [
        jnp.dot(query, keys, preferred_element_type=jnp.float32) * SCALE + bias for query, keys, bias in blocks
    ]
    tops = [jnp.max(score, axis=1, keepdims=True) for score in scores]
    weights = [jnp.exp(score - top) for score, top in zip(scores, tops)]
    totals = [jnp.sum(weight, axis=1, keepdims=True) for weight in weights]
    mixed = [
        lax.dot_general(
            weight.astype(jnp.bfloat16),
            keys[:KV_RANK],
            (((1,), (1,)), ((), ())),
            preferred_element_type=jnp.float32,
        )
        for weight, (_, keys, _) in zip(weights, blocks)
    ]
    return mixed, tops, totals


def resident_kernel(lengths, query, keys, out):
    item = pl.program_id(0)
    live = lax.broadcasted_iota(jnp.int32, (1, keys.shape[2]), 1) < lengths[item]
    bias = jnp.where(live, 0.0, DEAD)
    (mixed,), _, (total,) = weigh([(query[0].T, keys[0], bias)])
    out[0] = (mixed / total).astype(jnp.bfloat16)


def resident_rows(lengths, queries, cache):
    count, width, span = cache.shape
    heads = queries.shape[2]
    return pl.pallas_call(
        resident_kernel,
        out_shape=jax.ShapeDtypeStruct((queries.shape[0], heads, KV_RANK), jnp.bfloat16),
        grid_spec=pltpu.PrefetchScalarGridSpec(
            num_scalar_prefetch=1,
            grid=(count,),
            in_specs=[
                pl.BlockSpec((1, width, heads), lambda i, lengths: (i, 0, 0)),
                pl.BlockSpec((1, width, span), lambda i, lengths: (i, 0, 0)),
            ],
            out_specs=pl.BlockSpec((1, heads, KV_RANK), lambda i, lengths: (i, 0, 0)),
        ),
        compiler_params=pltpu.CompilerParams(vmem_limit_bytes=LARGE_VMEM),
        cost_estimate=pl.CostEstimate(
            flops=2 * count * heads * span * (width + KV_RANK),
            bytes_accessed=2 * count * width * span,
            transcendentals=count * heads * span,
        ),
        name="resident_rows",
    )(lengths, queries, cache)


def split_stat(row):
    high = row.astype(jnp.bfloat16).astype(jnp.float32)
    rest = row - high
    middle = rest.astype(jnp.bfloat16).astype(jnp.float32)
    return high, middle, rest - middle


def put_pair(out, values, rows):
    heads = rows[0].shape[1]
    line = lax.broadcasted_iota(jnp.int32, (STAT_ROWS, heads), 0)
    block = jnp.zeros((STAT_ROWS, heads), jnp.float32)
    for index in range(2):
        out[index * heads : (index + 1) * heads] = values[index].astype(out.dtype)
        for place, part in enumerate(split_stat(rows[index])):
            block = jnp.where(line == 3 * index + place, part, block)
    out[2 * heads :, :heads] = block.astype(out.dtype)
    out[2 * heads :, heads:] = jnp.zeros((STAT_ROWS, KV_RANK - heads), out.dtype)


def bias_kernel(span, meta, matching, lengths, bias):
    lane = lax.broadcasted_iota(jnp.int32, (1, span), 1)
    for half in range(2):
        slots = []
        for away in range(RING):
            z, y = meta[2], meta[3]
            if half == 0:
                y = (y + RING - away) & LAST
            else:
                z = (z + RING - away) & LAST
            slots.append(lane + (meta[1] * 16 + z * 4 + y) * span)
        slots = jnp.concatenate(slots, axis=1)
        for step in range(RING):
            for side in range(2):
                request = request_of(meta, matching, half, side, 0, step)
                live = slots < lengths[meta[0], request]
                row = (half * RING + step) * 2 + side
                bias[row : row + 1, :] = jnp.where(live, 0.0, DEAD)


def attention_bias(span, meta, matching, lengths):
    scalars = pl.BlockSpec(memory_space=pltpu.SMEM)
    return pl.pallas_call(
        functools.partial(bias_kernel, span),
        out_shape=pltpu.VMEM((4 * RING, RING * span), jnp.float32),
        in_specs=[scalars] * 3,
        out_specs=pl.BlockSpec(memory_space=pltpu.VMEM),
        compiler_params=pltpu.CompilerParams(vmem_limit_bytes=SMALL_VMEM),
        name="attention_bias",
    )(meta, matching, lengths)


def attend_ring(step, bias, a, b, queries, outs):
    blocks = []
    for half, segments in enumerate((a, b)):
        for side in range(2):
            row = (half * RING + step) * 2 + side
            keys = jnp.concatenate([segment[2 * step + side] for segment in segments], axis=1)
            blocks.append((queries[half][side][...].T, keys, bias[row : row + 1, :]))
    mixed, tops, totals = weigh(blocks)
    for half in range(2):
        pair = range(2 * half, 2 * half + 2)
        put_pair(
            outs[half],
            [mixed[index] / totals[index] for index in pair],
            [stat_row(tops[index], totals[index]) for index in pair],
        )


def stat_row(top, total):
    heads = top.shape[0]
    return jnp.broadcast_to(top + jnp.log(total), (heads, heads)).T[:1]


def partial_kernel(step, bias, *refs):
    a, b, plus, minus, outs = refs[:RING], refs[RING : 2 * RING], refs[8], refs[9], refs[10:]
    if step % 2:
        queries = [[ref.at[2 * RING + side] for side in range(2)] for ref in (b[RING - step], a[RING - step])]
    else:
        queries = [[plus.at[step + half], minus.at[step + half]] for half in range(2)]
    attend_ring(step, bias, a, b, queries, outs)


def partials(step, bias, arrays):
    width, span = arrays[0].shape[1:]
    heads = span
    work = 4 * heads * span * RING
    whole = pl.BlockSpec(memory_space=pltpu.VMEM)
    shape = (2 * heads + STAT_ROWS, KV_RANK)
    dtype = jnp.bfloat16 if step else jnp.float32
    return pl.pallas_call(
        functools.partial(partial_kernel, step),
        out_shape=[pltpu.VMEM(shape, dtype)] * 2,
        in_specs=[whole] * (1 + len(arrays)),
        out_specs=[whole] * 2,
        compiler_params=pltpu.CompilerParams(vmem_limit_bytes=SMALL_VMEM),
        cost_estimate=pl.CostEstimate(
            flops=2 * work * (width + KV_RANK),
            bytes_accessed=8 * RING * width * span,
            transcendentals=work,
        ),
        name="partials",
    )(bias, *arrays)


def merge(parts):
    heads = parts[0][0].shape[0]
    stats = [stat for _, stat in parts]
    top = functools.reduce(jnp.maximum, stats)
    shares = [jnp.exp(stat - top) for stat in stats]
    total = functools.reduce(jnp.add, shares)
    mixed = 0.0
    for (value, _), share in zip(parts, shares):
        column = jnp.broadcast_to(share / total, (heads, heads)).T[:, :1]
        mixed = mixed + value * column
    return mixed, top + jnp.log(total)


def received(pair, index):
    heads = (pair.shape[0] - STAT_ROWS) // 2
    rows = pair[2 * heads :, :heads].astype(jnp.float32)
    values = pair[index * heads : (index + 1) * heads].astype(jnp.float32)
    first = 3 * index
    return values, rows[first : first + 1] + rows[first + 1 : first + 2] + rows[first + 2 : first + 3]


def middle_kernel(*refs):
    ins, outs = refs[: 2 * RING], refs[2 * RING :]
    for side in range(2):
        merged = [merge([received(ref, side) for ref in ins[half * RING : (half + 1) * RING]]) for half in range(2)]
        put_pair(outs[side], [mixed for mixed, _ in merged], [row for _, row in merged])


def middle(parts):
    whole = pl.BlockSpec(memory_space=pltpu.VMEM)
    return pl.pallas_call(
        middle_kernel,
        out_shape=[pltpu.VMEM(parts[-1].shape, jnp.bfloat16)] * 2,
        in_specs=[whole] * (2 * RING),
        out_specs=[whole] * 2,
        compiler_params=pltpu.CompilerParams(vmem_limit_bytes=SMALL_VMEM),
        name="middle",
    )(*parts)


def last_kernel(base, plus, minus, out):
    del base
    for half in range(2):
        mixed, _ = merge([received(plus, half), received(minus, half)])
        out[half] = mixed.astype(jnp.bfloat16)


def last(base, plus, minus):
    count, heads, rank = base.shape
    whole = pl.BlockSpec(memory_space=pltpu.VMEM)
    return pl.pallas_call(
        last_kernel,
        out_shape=jax.ShapeDtypeStruct(base.shape, base.dtype),
        grid=(1,),
        in_specs=[pl.BlockSpec(memory_space=pl.ANY), whole, whole],
        out_specs=pl.BlockSpec((count // 2, heads, rank), lambda i: (1, 0, 0)),
        input_output_aliases={0: 0},
        compiler_params=pltpu.CompilerParams(vmem_limit_bytes=SMALL_VMEM),
        name="last",
    )(base, plus, minus)


def per_device(queries, res_cache, res_lengths, inc_cache, inc_lengths, matching):
    meta = positions()
    queries = jnp.swapaxes(queries[0], 1, 2)
    res_cache = jnp.swapaxes(res_cache[0], 1, 2)
    inc_cache = jnp.swapaxes(inc_cache[0], 1, 2)

    far_a = move(queries[2:3], dz=2)
    far_b = move(queries[3:4], dy=2)
    a2, b2 = gather_requests(((0, 2), (1, 2)), 0, meta, matching, inc_cache)
    a2, b2, far_a, far_b = lax.optimization_barrier((a2, b2, far_a, far_b))
    a2 = move(a2, dy=2)
    b2 = move(b2, dz=2)
    packed = pack_queries(queries, far_a, far_b)
    from_minus = move(packed, dx=1)
    from_plus = move(packed, dx=-1)
    sent = gather_requests(((0, 1), (0, 3), (1, 1), (1, 3)), 2, meta, matching, inc_cache)
    a1, a3, b1, b3 = fill_queries((1, 1, 0, 0), sent, from_plus, from_minus)
    a1 = move(a1, dy=1)
    b1 = move(b1, dz=1)
    a3 = move(a3, dy=-1)
    b3, a2, b2, lengths = lax.optimization_barrier((b3, a2, b2, res_lengths[0]))
    b3 = move(b3, dz=-1)
    base = resident_rows(lengths, queries, res_cache)
    later, base = lax.optimization_barrier((meta, base))
    a0, b0 = gather_requests(((0, 0), (1, 0)), 0, later, matching, inc_cache)

    arrays = (a0, a1, a2, a3, b0, b1, b2, b3, from_plus, from_minus)
    pa, pb = [], []
    order = attention_bias(inc_cache.shape[2], later, matching, inc_lengths)
    for step in (2, 3, 1, 0):
        for_a, for_b = partials(step, order, arrays)
        order, for_a, for_b = lax.optimization_barrier((order, for_a, for_b))
        pa.append(move(for_a, dz=step) if step else for_a)
        pb.append(move(for_b, dy=step) if step else for_b)
    to_plus, to_minus = middle(pa + pb)
    plus = move(to_plus, dx=1)
    minus = move(to_minus, dx=-1)
    return last(base, plus, minus)[None]


def solution(mesh):
    placed = (
        P("section", "dev", None, None),
        P("section", "dev", None, None),
        P("section", "dev"),
        P("section", None, "dev", None),
        P(),
        P(),
    )
    return jax.shard_map(
        per_device,
        mesh=mesh,
        in_specs=placed,
        out_specs=P("section", "dev", None, None),
        check_vma=False,
    )
```
